128 devices in a mesh: tile: 32 (over x_hi, y, z), chan: 4 (over x_lo, core).
Axes of the slice: x: 4 (x_hi: 2, x_lo: 2; x = x_hi * 2 + x_lo), y: 4, z: 4, core: 2. Of those that a mesh axis runs over, the one named last changes fastest.
Arguments:
- video: bfloat16 [128, 384, 16, 128], P('tile', 'chan'), may hold values from -30 to 30
- clip_lengths: int32 [32], replicated, may hold values from 1 to 16, 128 in all
- norm_gain: float32 [384], P('chan'), may hold values from 0.5 to 1.5
- norm_shift: float32 [384], P('chan'), may hold values from -3 to 3
- conv_weight: bfloat16 [3, 3, 3, 384, 384], P(None, None, None, None, 'chan'), may hold values from -0.0625 to 0.0625
- conv_bias: float32 [384], P('chan'), may hold values from -3 to 3
Outputs:
- block_out: bfloat16 [128, 384, 16, 128], P('tile', 'chan')
The draws below stay inside these ranges and needn't reach their ends.
Inputs may be any that keep to these rules, and one draw needn't show every extreme that they name: `clip_lengths`: the clips fill all 128 frames; the longest has exactly 16 frames.
All inputs are finite; a program needn't handle non-finite values.
Results may differ from the reference program's by a relative error of at most 0.0017.
Values may be sent and summed in bfloat16 or wider, within the bound.
A program may use at most 256 MiB of HBM per device.

```python
import math
import jax
import jax.numpy as jnp
import numpy as np
from jax import lax

C = 384
GROUPS = 32
H = 16
W = 128
FRAMES = 128
CLIPS = 32
MOST = 16


def draw_video(key, part):
    key = jax.random.fold_in(key, 11)
    key_base = jax.random.fold_in(key, 0)
    key_chan = jax.random.fold_in(key, 1)
    key_gain = jax.random.fold_in(key, 3)
    key_offset = jax.random.fold_in(key, 4)
    key_freq = jax.random.fold_in(key, 5)
    key_phase = jax.random.fold_in(key, 6)
    shape = (FRAMES, C, H, W)
    base = jnp.clip(jax.random.normal(key_base, shape, jnp.float32), -4.0, 4.0)
    offset_rough = 1.2
    offset_smooth = 1.2
    frame_pos = jnp.arange(FRAMES, dtype=jnp.float32)
    rising = jnp.exp(jnp.log(3.0) * frame_pos / float(FRAMES - 1))
    frame_gain = jnp.exp(jax.random.uniform(key_gain, (FRAMES,), jnp.float32, jnp.log(0.5), jnp.log(1.6)))
    chan_scale = jnp.exp(jax.random.uniform(key_chan, (C,), jnp.float32, jnp.log(0.5), jnp.log(2.0)))
    freq = jax.random.uniform(key_freq, (1, GROUPS), jnp.float32, 0.2, 0.9)
    phase = jax.random.uniform(key_phase, (1, GROUPS), jnp.float32, -3.14159, 3.14159)
    drift = offset_smooth * jnp.sin(frame_pos[:, None] * freq + phase)
    rough = offset_rough * jnp.clip(jax.random.normal(key_offset, (FRAMES, GROUPS), jnp.float32), -3.0, 3.0)
    offset = (drift + rough) * rising[:, None]
    offset = jnp.repeat(offset, C // GROUPS, axis=1)
    local_scale = (rising * frame_gain)[:, None] * chan_scale[None, :]
    values = base * local_scale[:, :, None, None] + offset[:, :, None, None]
    return jnp.clip(values, -30.0, 30.0).astype(jnp.bfloat16)


def shard_levels(rng, extent, shards, low, largest):
    def one(dim, parts):
        heights = jax.random.uniform(jax.random.fold_in(jax.random.fold_in(rng, 6), dim), (parts,), jnp.float32, low / len(shards), largest / len(shards))
        return jnp.repeat(jnp.exp(heights), extent[dim] // parts).reshape((-1,) + (1,) * (len(extent) - dim - 1))

    gain = one(*shards[0])
    for cut in shards[1:]:
        gain = gain * one(*cut)
    return gain


def profile(number_of, total, most, lean):
    loads = [(1 << 20) // math.isqrt(standing ** lean) + 1 for standing in range(2, number_of + 1)]
    spare, counts = total - most - (number_of - 1), [1] * (number_of - 1)
    while spare > 0:
        free = [i for i in range(number_of - 1) if counts[i] < most]
        pool, budget = sum([loads[i] for i in free]), spare
        for i in free:
            more = min(most - counts[i], max(1, budget * loads[i] // pool), spare)
            counts[i] = counts[i] + more
            spare = spare - more
    return np.array([most] + counts)


def ragged(rng, count, total, bound, skew):
    if count == 2:
        one = jax.random.randint(rng, (), max(1, total - bound), min(bound, total - 1) + 1)
        return jnp.stack([one, total - one])
    tallies = jnp.asarray(profile(count, total, bound, skew), jnp.int32)
    twos = (count - 1) // 2
    donor, taker = tallies[1:1 + 2 * twos:2], tallies[2:2 + 2 * twos:2]
    margin = jnp.minimum(donor - 1, bound - taker)
    moved = jax.random.randint(jax.random.fold_in(rng, 1), (twos,), 0, 1 << 20) % (margin + 1)
    tallies = tallies.at[1:1 + 2 * twos:2].set(donor - moved).at[2:2 + 2 * twos:2].set(taker + moved)
    return tallies[jax.random.permutation(jax.random.fold_in(rng, 2), count)]


def gaussian(stream_key, dims, scale, limit, cuts=(), kind=jnp.bfloat16):
    entries = jax.random.normal(stream_key, dims, jnp.float32) * scale
    if len(cuts) > 0:
        entries = shard_levels(stream_key, dims, cuts, -0.22, 0.18) * entries
    return jnp.clip(entries, min=-limit, max=limit).astype(kind)


def setup_inputs(seed: int = 0) -> dict:
    seeds = jax.random.split(jax.random.key(seed), 7)
    video = draw_video(jax.random.fold_in(seeds[6], 71), 0)
    clip_lengths = ragged(seeds[1], CLIPS, FRAMES, MOST, 2).astype(jnp.int32)
    norm_gain = jnp.clip(0.5 + 1.0 * jax.random.uniform(seeds[2], (C,), jnp.float32) ** shard_levels(seeds[2], (C,), ((0, 4),), -0.2, 0.2), 0.5, 1.5)
    norm_shift = gaussian(seeds[3], (C,), 0.5, 3.0, ((0, 4),), jnp.float32)
    conv_weight = gaussian(seeds[4], (3, 3, 3, C, C), (27 * C) ** -0.5, 0.0625, ((4, 4),))
    conv_bias = gaussian(seeds[5], (C,), 0.5, 3.0, ((0, 4),), jnp.float32)
    return dict(video=video, clip_lengths=clip_lengths, norm_gain=norm_gain, norm_shift=norm_shift, conv_weight=conv_weight, conv_bias=conv_bias)


def reference(video, clip_lengths, norm_gain, norm_shift, conv_weight, conv_bias):
    hi = lax.Precision.HIGHEST
    x = video.astype(jnp.float32)
    ends = jnp.cumsum(clip_lengths).astype(jnp.int32)
    starts = (ends - clip_lengths).astype(jnp.int32)
    frame = jnp.arange(FRAMES, dtype=jnp.int32)
    inside = (frame[:, None] >= starts[None, :]) & (frame[:, None] < ends[None, :])
    member = inside.astype(jnp.float32)
    start_of = lax.optimization_barrier(jnp.sum(jnp.where(inside, starts[None, :], 0), axis=1)).astype(jnp.int32)
    grouped = x.reshape(FRAMES, GROUPS, C // GROUPS, H, W)
    count = clip_lengths.astype(jnp.float32) * float(C // GROUPS * H * W)
    frame_sum = lax.optimization_barrier(jnp.sum(grouped, axis=(2, 3, 4)))
    mean_clip = jnp.dot(member.T, frame_sum, precision=hi) / count[:, None]
    mean_frame = jnp.dot(member, mean_clip, precision=hi)
    centered = grouped - mean_frame[:, :, None, None, None]
    frame_sq = lax.optimization_barrier(jnp.sum(centered * centered, axis=(2, 3, 4)))
    spread_clip = jnp.dot(member.T, frame_sq, precision=hi) / count[:, None]
    scale_frame = jnp.dot(member, lax.rsqrt(spread_clip + 1e-06), precision=hi)
    normed = (centered * scale_frame[:, :, None, None, None]).reshape(FRAMES, C, H, W)
    normed = normed * norm_gain[None, :, None, None] + norm_shift[None, :, None, None]
    hidden = jax.nn.silu(normed).astype(jnp.bfloat16)
    total = jnp.zeros((FRAMES, C, H, W), jnp.float32)
    for tap in range(3):
        back = 2 - tap
        if back > 0:
            shifted = jnp.concatenate([jnp.zeros((back, C, H, W), hidden.dtype), hidden[:FRAMES - back]], axis=0)
        else:
            shifted = hidden
        valid = frame - back >= start_of
        shifted = jnp.where(valid[:, None, None, None], shifted, jnp.zeros_like(shifted))
        total = total + lax.conv_general_dilated(shifted, conv_weight[tap], (1, 1), ((1, 1), (1, 1)), dimension_numbers=('NCHW', 'HWIO', 'NCHW'), preferred_element_type=jnp.float32)
    return (x + total + conv_bias[None, :, None, None]).astype(jnp.bfloat16)
```

```python
import jax
import jax.numpy as jnp
from jax import lax
from jax.experimental import pallas as pl
from jax.experimental.pallas import tpu as pltpu
from jax.sharding import PartitionSpec as P

MESH = pl.DeviceIdType.MESH
F32 = jnp.float32
BF16 = jnp.bfloat16
PER_GROUP = 12
HOPS = (1, -1, 2, -2, 3, -3, 4, -4)
EPS = 1e-06


def swap_matrix():
    row = lax.broadcasted_iota(jnp.int32, (256, 256), 0)
    col = lax.broadcasted_iota(jnp.int32, (256, 256), 1)
    return jnp.where(col == (row % 16) * 16 + row // 16, 1.0, 0.0).astype(BF16)


def kernel(
    lens, gain, shift, bias, video, weight, out,
    raw_own, raw_sib, raw_x, raw_xs, slab, wt, hid_a, hid_b, acc, pout, pin, obuf, ab, abmsg, par, swap, srow, mrow, stat, msk,
    own_sem, w_sem, out_sem, xs, xr, ss, sr, fs, fr, ts, tr, cs, cr, ps, pr,
):
    frames, chans, rows, cols = video.shape
    groups = chans // PER_GROUP
    half = chans // 2
    kdim = 9 * 2 * chans
    row_k = 3 * 2 * chans
    t, c = lax.axis_index("tile"), lax.axis_index("chan")
    tiles = lax.axis_size("tile")

    def tile_at(hop):
        return (lax.rem(t + hop + tiles, tiles), c)

    def mate(r):
        return (t, c + r - 2 * (c % 2) if r == 1 else c + 2 - 4 * (c // 2) if r == 2 else 3 - c)

    def remote(src, dst, send, recv, dev):
        return pltpu.make_async_remote_copy(
            src_ref=src, dst_ref=dst, send_sem=send, recv_sem=recv, device_id=dev, device_id_type=MESH
        )

    def half_frame(k):
        return pl.ds((k % 2) * half, half)

    def to_x(k):
        f, here = k // 2, half_frame(k)
        return remote(video.at[f, here], raw_x.at[f, here], xs.at[k], xr.at[k], mate(2))

    def to_sibling(f):
        return remote(video.at[f], raw_sib.at[f], ss.at[f], sr.at[f], mate(1))

    def forward(k):
        f, here = k // 2, half_frame(k)
        return remote(raw_x.at[f, here], raw_xs.at[f, here], fs.at[k], fr.at[k], mate(1))

    def send_stat(i):
        return remote(stat.at[8], stat.at[i], ts.at[i], tr.at[i], tile_at(HOPS[i]))

    def send_ab(r):
        return remote(abmsg.at[0], abmsg.at[r], cs.at[r], cr.at[r], mate(r))

    def send_part(i):
        return remote(pout.at[i], pin.at[i], ps.at[i], pr.at[i], (lax.rem(t + 1, tiles), c))

    def own_copy(f):
        return pltpu.make_async_copy(video.at[f], raw_own.at[f], own_sem.at[f])

    def out_copy(f):
        return pltpu.make_async_copy(obuf.at[f], out.at[f], out_sem.at[f])

    def w_copy(dt):
        return pltpu.make_async_copy(weight.at[dt], slab.at[dt], w_sem.at[dt])

    for f in range(frames):
        own_copy(f).start()
    barrier = pltpu.get_barrier_semaphore()
    neighbours = [tile_at(h) for h in HOPS] + [mate(r) for r in (1, 2, 3)]
    for d in neighbours:
        pl.semaphore_signal(barrier, inc=1, device_id=d, device_id_type=MESH)
    pl.semaphore_wait(barrier, len(neighbours))
    order = [2 * f + j for f in reversed(range(frames)) for j in range(2)]
    for k in order[:3]:
        to_x(k).start()
    for f in reversed(range(frames)):
        to_sibling(f).start()
    for dt in range(3):
        w_copy(dt).start()

    for f in range(frames):
        own_copy(f).wait()
    count = float(PER_GROUP * rows * cols)

    def sums(i, _):
        x = raw_own[i // groups, pl.ds((i % groups) * PER_GROUP, PER_GROUP)].astype(F32)
        srow[pl.ds(i, 1), :] = jnp.sum(jnp.sum(x, axis=0), axis=0, keepdims=True)
        return _

    lax.fori_loop(0, frames * groups, sums, 0)
    mrow[...] = jnp.broadcast_to(jnp.sum(srow[...], axis=1, keepdims=True) / count, mrow.shape)

    def squares(i, _):
        x = raw_own[i // groups, pl.ds((i % groups) * PER_GROUP, PER_GROUP)].astype(F32)
        d = x - mrow[pl.ds(i, 1), :][None]
        srow[pl.ds(i, 1), :] = jnp.sum(jnp.sum(d * d, axis=0), axis=0, keepdims=True)
        return _

    lax.fori_loop(0, frames * groups, squares, 0)
    sq = jnp.broadcast_to(jnp.sum(srow[...], axis=1, keepdims=True), srow.shape)
    lane = lax.broadcasted_iota(jnp.int32, (groups, cols), 1)
    message = jnp.zeros((groups, cols), F32)
    for f in range(frames):
        here = slice(f * groups, (f + 1) * groups)
        message = jnp.where(lane // 16 == f, mrow[here, :], message)
        message = jnp.where(lane // 16 == frames + f, sq[here], message)
    stat[8] = message
    for i, hop in enumerate(HOPS):

        @pl.when((t + hop >= 0) & (t + hop < tiles))
        def _():
            send_stat(i).start()


    first = t * frames

    def bounds(k, carry):
        end, starts, ends = carry
        end = end + lens[k]
        starts = tuple(jnp.where(end <= first + f, end, starts[f]) for f in range(frames))
        ends = tuple(jnp.where(end > first + f, jnp.minimum(ends[f], end), ends[f]) for f in range(frames))
        return end, starts, ends

    zero = jnp.int32(0)
    _, starts, ends = lax.fori_loop(
        0, lens.shape[0], bounds, (zero, (zero,) * frames, (jnp.int32(1 << 20),) * frames)
    )
    for f in range(frames):
        for dt in range(3):
            msk[f * 3 + dt] = jnp.where(first + f + 2 - dt < ends[f], 1.0, 0.0).astype(F32)

    def spread_rows(k, _):
        par[0, pl.ds(k, 1), :] = jnp.full((1, cols), gain[k], F32)
        par[1, pl.ds(k, 1), :] = jnp.full((1, cols), shift[k], F32)
        par[2, pl.ds(k, 1), :] = jnp.full((1, cols), bias[k], F32)
        return _

    lax.fori_loop(0, chans, spread_rows, 0)
    swap[...] = swap_matrix()

    for part in range(2):
        acc[frames + part] = jnp.zeros((rows, chans, cols), F32)

    def tiles_of(ref, at):
        return jnp.concatenate([ref[(*at, pl.ds(16 * j, 16))].reshape(256, cols) for j in range(chans // 16)], axis=1)

    def begin(f, _):
        y = jnp.dot(swap[...], tiles_of(raw_own, (f,)), preferred_element_type=F32)
        for j in range(chans // 16):
            here = slice(16 * j, 16 * (j + 1))
            acc[f, :, here, :] = y[:, j * cols : (j + 1) * cols].reshape(rows, 16, cols) + par[2, here, :][None]
        return _

    lax.fori_loop(0, frames, begin, 0)

    for dt in range(3):
        w_copy(dt).wait()
        for q in range(2):
            for tap in range(9):
                wt[q, dt * chans : (dt + 1) * chans, tap * 2 * chans : (tap + 1) * 2 * chans] = slab[
                    dt, tap, :, q * 2 * chans : (q + 1) * 2 * chans
                ]

    for hid in (hid_a, hid_b):
        hid[0:row_k, :] = jnp.zeros((row_k, cols), BF16)
        hid[17 * row_k : 18 * row_k, :] = jnp.zeros((row_k, cols), BF16)

    for i, hop in enumerate(HOPS):

        @pl.when((t - hop >= 0) & (t - hop < tiles))
        def _():
            send_stat(i).wait_recv()

    lane_frame = (lane // 16) % frames
    is_mean = lane // 16 < frames
    scales = jnp.zeros((chans, cols), F32)
    lane_c = lax.broadcasted_iota(jnp.int32, (chans, cols), 1)
    row8 = lax.broadcasted_iota(jnp.int32, (8, cols), 0)

    def per_channel(v):
        blocks = []
        for b in range(chans // 8):
            g0, g1 = (8 * b) // PER_GROUP, (8 * b + 7) // PER_GROUP
            lo = jnp.broadcast_to(v[g0 : g0 + 1], (8, cols))
            if g1 != g0:
                lo = jnp.where(row8 < (g0 + 1) * PER_GROUP - 8 * b, lo, jnp.broadcast_to(v[g1 : g1 + 1], (8, cols)))
            blocks.append(lo)
        return jnp.concatenate(blocks, axis=0)

    hops = (*HOPS, 0)
    for f in range(frames):
        inside = []
        for h in hops:
            at = (t - h) * frames + lane_frame
            inside.append((at >= starts[f]) & (at < ends[f]))
        length = (ends[f] - starts[f]).astype(F32)
        total = jnp.zeros((groups, cols), F32)
        for i in range(9):
            total = total + jnp.where(inside[i] & is_mean, stat[i], 0.0)
        mean = jnp.sum(total, axis=1, keepdims=True) / (16.0 * length)
        total = jnp.zeros((groups, cols), F32)
        for i in range(9):
            d = stat[i] - mean
            total = total + jnp.where(inside[i], jnp.where(is_mean, d * d, stat[i] * (1.0 / count)), 0.0)
        spread = jnp.sum(total, axis=1, keepdims=True) / (16.0 * length)
        rstd = lax.rsqrt(spread + EPS)
        a = 0.5 * (per_channel(jnp.broadcast_to(rstd, (groups, cols))) * par[0])
        b = 0.5 * par[1] - per_channel(jnp.broadcast_to(mean, (groups, cols))) * a
        ab[0, 0, f] = a
        ab[0, 1, f] = b
        scales = jnp.where(lane_c // 16 == f, a, scales)
        scales = jnp.where(lane_c // 16 == frames + f, b, scales)
    abmsg[0] = scales
    for r in (2, 3, 1):
        send_ab(r).start()
    for k in order[3:]:
        to_x(k).start()

    def expand(r):
        for f in range(frames):
            ab[r, 0, f] = jnp.broadcast_to(abmsg[r, :, 16 * f : 16 * f + 1], (chans, cols))
            lo = 16 * (frames + f)
            ab[r, 1, f] = jnp.broadcast_to(abmsg[r, :, lo : lo + 1], (chans, cols))

    lane_t = lax.broadcasted_iota(jnp.int32, (16, cols), 1)

    def normalize(slot, f, hid, place):
        y = jnp.dot(swap[...], tiles_of((raw_own, raw_sib, raw_x, raw_xs)[slot], (f,)), preferred_element_type=F32)
        for j in range(chans // 16):
            here = slice(16 * j, 16 * (j + 1))
            a, b = ab[slot, 0, f, here, :], ab[slot, 1, f, here, :]
            for h in range(rows):
                z = y[h * 16 : (h + 1) * 16, j * cols : (j + 1) * cols] * a + b
                z = z + z * jnp.tanh(z)
                left = jnp.where(lane_t == 0, 0.0, pltpu.roll(z, 1, 1))
                right = jnp.where(lane_t == cols - 1, 0.0, pltpu.roll(z, cols - 1, 1))
                for dw, piece in enumerate((left, z, right)):
                    to = pl.multiple_of(((h + 1) * 3 + dw) * 2 * chans + place * chans + 16 * j, 16)
                    hid[pl.ds(to, 16), :] = piece.astype(BF16)

    def convolve(q, f, hid, first_row, n):
        pieces = [hid[pl.ds(pl.multiple_of((first_row + j) * row_k, row_k), kdim), :] for j in range(n)]
        res = jnp.dot(wt[q], jnp.concatenate(pieces, axis=1), preferred_element_type=F32)
        for dt in range(3):
            m = msk[f * 3 + dt]
            for j in range(n):
                part = res[dt * chans : (dt + 1) * chans, j * cols : (j + 1) * cols]
                acc[f + 2 - dt, first_row + j] += part * m

    def stage(conv, norm):
        n = rows // 2

        for p in range(2):
            if conv is not None:
                q, f = conv
                convolve(q + (1 - 2 * q) * (c // 2), f, hid_of[conv], p * n, n)
            if norm is not None:
                q, f = norm
                normalize(2 * q + p, f, hid_of[norm], p + (1 - 2 * p) * (c % 2))

    def finish(f):
        pieces = []
        for j in range(chans // 16):
            here = slice(16 * j, 16 * (j + 1))
            value = acc[f, :, here, :]
            pieces.append(value.astype(BF16).reshape(256, cols))
        y = jnp.dot(swap[...], jnp.concatenate(pieces, axis=1), preferred_element_type=F32).astype(BF16)
        for j in range(chans // 16):
            obuf[f, 16 * j : 16 * (j + 1)] = y[:, j * cols : (j + 1) * cols].reshape(16, rows, cols)
        out_copy(f).start()

    def arrived(f):
        for k in (2 * f, 2 * f + 1):
            to_x(k).wait_recv()
            forward(k).start()

    def forwarded(f):
        for k in (2 * f, 2 * f + 1):
            forward(k).wait_recv()

    def send_halo(i):
        @pl.when(t < tiles - 1)
        def _():
            pout[i] = acc[frames + i].astype(BF16)
            send_part(i).start()

    own, rem = 0, 1
    steps = [(own, 3), (own, 2), (rem, 3), (own, 1), (rem, 2), (own, 0), (rem, 1), (rem, 0)]
    hid_of = {step: (hid_a, hid_b)[i % 2] for i, step in enumerate(steps)}

    send_ab(1).wait_recv()
    expand(1)
    for f in range(frames):
        to_sibling(f).wait_recv()
    with jax.named_scope("norm_first"):
        stage(None, (own, 3))
    with jax.named_scope("own3"):
        stage((own, 3), (own, 2))
    arrived(3)
    send_ab(2).wait_recv()
    expand(2)
    send_ab(3).wait_recv()
    expand(3)
    forwarded(3)
    with jax.named_scope("own2"):
        stage((own, 2), (rem, 3))
    with jax.named_scope("rem3"):
        stage((rem, 3), (own, 1))
    send_halo(1)
    with jax.named_scope("wait2"):
        arrived(2)
        forwarded(2)
    with jax.named_scope("own1"):
        stage((own, 1), (rem, 2))
    with jax.named_scope("rem2"):
        stage((rem, 2), (own, 0))
    send_halo(0)
    with jax.named_scope("wait1"):
        arrived(1)
        forwarded(1)
    with jax.named_scope("own0"):
        stage((own, 0), (rem, 1))
    with jax.named_scope("rem1"):
        stage((rem, 1), None)
    finish(3)
    with jax.named_scope("wait0"):
        arrived(0)
        forwarded(0)
    with jax.named_scope("norm_last"):
        stage(None, (rem, 0))
    with jax.named_scope("rem0"):
        stage((rem, 0), None)
    with jax.named_scope("finish"):
        finish(2)
        for i in range(2):

            @pl.when(t > 0)
            def _():
                send_part(1 - i).wait_recv()
                acc[1 - i] += pin[1 - i].astype(F32)

            finish(1 - i)

    for i in range(2):

        @pl.when(t < tiles - 1)
        def _():
            send_part(i).wait_send()

    for f in range(frames):
        out_copy(f).wait()
        to_sibling(f).wait_send()
    for k in order:
        to_x(k).wait_send()
        forward(k).wait_send()
    for i, hop in enumerate(HOPS):

        @pl.when((t + hop >= 0) & (t + hop < tiles))
        def _():
            send_stat(i).wait_send()

    for r in (1, 2, 3):
        send_ab(r).wait_send()


def on_device(video, clip_lengths, norm_gain, norm_shift, conv_weight, conv_bias):
    frames, chans, rows, cols = video.shape
    groups = chans // PER_GROUP
    all_chans = conv_weight.shape[3]
    weight = jnp.swapaxes(conv_weight, 3, 4).reshape(3, 9, chans, all_chans)
    dma = pltpu.SemaphoreType.DMA
    smem, anyspace = pl.BlockSpec(memory_space=pltpu.SMEM), pl.BlockSpec(memory_space=pl.ANY)
    return pl.pallas_call(
        kernel,
        out_shape=jax.ShapeDtypeStruct(video.shape, BF16),
        in_specs=[smem] * 4 + [anyspace] * 2,
        out_specs=anyspace,
        scratch_shapes=[
            pltpu.VMEM((frames, chans, rows, cols), BF16),
            pltpu.VMEM((frames, chans, rows, cols), BF16),
            pltpu.VMEM((frames, chans, rows, cols), BF16),
            pltpu.VMEM((frames, chans, rows, cols), BF16),
            pltpu.VMEM((3, 9, chans, 4 * chans), BF16),
            pltpu.VMEM((2, 3 * chans, 18 * chans), BF16),
            pltpu.VMEM((18 * 6 * chans, cols), BF16),
            pltpu.VMEM((18 * 6 * chans, cols), BF16),
            pltpu.VMEM((frames + 2, rows, chans, cols), F32),
            pltpu.VMEM((2, rows, chans, cols), BF16),
            pltpu.VMEM((2, rows, chans, cols), BF16),
            pltpu.VMEM((frames, chans, rows, cols), BF16),
            pltpu.VMEM((4, 2, frames, chans, cols), F32),
            pltpu.VMEM((4, chans, cols), F32),
            pltpu.VMEM((3, chans, cols), F32),
            pltpu.VMEM((256, 256), BF16),
            pltpu.VMEM((frames * groups, cols), F32),
            pltpu.VMEM((frames * groups, cols), F32),
            pltpu.VMEM((9, groups, cols), F32),
            pltpu.SMEM((3 * frames,), F32),
            dma((frames,)), dma((3,)), dma((frames,)),
            dma((2 * frames,)), dma((2 * frames,)), dma((frames,)), dma((frames,)), dma((2 * frames,)), dma((2 * frames,)),
            dma((8,)), dma((8,)), dma((4,)), dma((4,)), dma((2,)), dma((2,)),
        ],
        compiler_params=pltpu.CompilerParams(
            collective_id=0, has_side_effects=True, vmem_limit_bytes=60 << 20
        ),
        name="resblock",
    )(clip_lengths, norm_gain, norm_shift, conv_bias, video, weight)


def solution(mesh):
    return jax.shard_map(
        on_device,
        mesh=mesh,
        in_specs=(
            P("tile", "chan", None, None),
            P(),
            P("chan"),
            P("chan"),
            P(None, None, None, None, "chan"),
            P("chan"),
        ),
        out_specs=P("tile", "chan", None, None),
        check_vma=False,
    )
```

```python
import jax
import jax.numpy as jnp
from jax import lax
from jax.experimental import pallas as pl
from jax.experimental.pallas import tpu as pltpu
from jax.sharding import PartitionSpec as P

MESH = pl.DeviceIdType.MESH
F32 = jnp.float32
BF16 = jnp.bfloat16
PER_GROUP = 12
HOPS = (1, -1, 2, -2, 3, -3, 4, -4)
EPS = 1e-06
RELAYS = 8


def swap_matrix():
    row = lax.broadcasted_iota(jnp.int32, (256, 256), 0)
    col = lax.broadcasted_iota(jnp.int32, (256, 256), 1)
    return jnp.where(col == (row % 16) * 16 + row // 16, 1.0, 0.0).astype(BF16)


def kernel(
    lens_in, gain_in, shift_in, bias_in, video, weight, out,
    raw_own, raw_sib, raw_x, raw_xs, slab, wt, hid_a, hid_b, acc, pout, pin, hop_buf, ab, abmsg, par, swap, srow, mrow, stat, msk, lens, gain, shift, bias, par_sem,
    own_sem, w_sem, xs, xr, ss, sr, fs, fr, ts, tr, cs, cr, ps, pr, hs, hr, qs, qr,
):
    frames, chans, rows, cols = video.shape
    groups = chans // PER_GROUP
    half = chans // 2
    kdim = 9 * 2 * chans
    row_k = 3 * 2 * chans
    t, c = lax.axis_index("tile"), lax.axis_index("chan")
    tiles = lax.axis_size("tile")

    def tile_at(hop):
        return (lax.rem(t + hop + tiles, tiles), c)

    def mate(r):
        return (t, c + r - 2 * (c % 2) if r == 1 else c + 2 - 4 * (c // 2) if r == 2 else 3 - c)

    def remote(src, dst, send, recv, dev):
        return pltpu.make_async_remote_copy(
            src_ref=src, dst_ref=dst, send_sem=send, recv_sem=recv, device_id=dev, device_id_type=MESH
        )

    def half_frame(k):
        return pl.ds((k % 2) * half, half)

    def to_x(k):
        f, here = k // 2, half_frame(k)
        return remote(video.at[f, here], raw_x.at[f, here], xs.at[k], xr.at[k], mate(2))

    def to_sibling(f):
        return remote(video.at[f], raw_sib.at[f], ss.at[f], sr.at[f], mate(1))

    def forward(k):
        f, here = k // 2, half_frame(k)
        return remote(raw_x.at[f, here], raw_xs.at[f, here], fs.at[k], fr.at[k], mate(1))

    def send_stat(i):
        return remote(stat.at[8], stat.at[i], ts.at[i], tr.at[i], tile_at(HOPS[i]))

    def send_ab(r):
        return remote(abmsg.at[0], abmsg.at[r], cs.at[r], cr.at[r], mate(r))

    def send_part(i):
        return remote(pout.at[i], pin.at[i], ps.at[i], pr.at[i], (lax.rem(t + 1, tiles), c))

    cross = tiles // 2 - 1
    first_relay = cross - 10
    from_first = t - first_relay
    is_relay = (from_first >= 0) & (from_first < 10) & ((from_first + tiles) % 4 < 3)
    my_share = from_first - from_first // 4
    share = rows // RELAYS

    def relay(j):
        return (first_relay + 4 * (j // 3) + j % 3, c)

    def to_relay(i, j):
        src = pout.at[i, pl.ds(j * share, share)]
        return remote(src, hop_buf.at[i], hs.at[i, j], hr.at[i], relay(j))

    def from_relay(i, j):
        dst = pin.at[i, pl.ds(j * share, share)]
        return remote(hop_buf.at[i], dst, qs.at[i], qr.at[i, j], (cross + 1, c))

    def own_copy(f):
        return pltpu.make_async_copy(video.at[f], raw_own.at[f], own_sem.at[f])

    def w_copy(dt):
        return pltpu.make_async_copy(weight.at[dt], slab.at[dt], w_sem.at[dt])

    small = [
        pltpu.make_async_copy(src, dst, par_sem.at[i])
        for i, (src, dst) in enumerate(((lens_in, lens), (gain_in, gain), (shift_in, shift), (bias_in, bias)))
    ]
    for f in range(frames):
        own_copy(f).start()
    for copy in small:
        copy.start()
    barrier = pltpu.get_barrier_semaphore()
    for r in (2, 1, 3):
        pl.semaphore_signal(barrier, inc=1, device_id=mate(r), device_id_type=MESH)
    for hop in HOPS:

        @pl.when((t + hop >= 0) & (t + hop < tiles))
        def _():
            pl.semaphore_signal(barrier, inc=1, device_id=tile_at(hop), device_id_type=MESH)

    @pl.when((t == cross) | (t == cross + 1))
    def _():
        for j in range(RELAYS):
            pl.semaphore_signal(barrier, inc=1, device_id=relay(j), device_id_type=MESH)

    @pl.when(is_relay)
    def _():
        for d in (cross, cross + 1):
            pl.semaphore_signal(barrier, inc=1, device_id=(d, c), device_id_type=MESH)

    peers = 3 + jnp.minimum(t, 4) + jnp.minimum(tiles - 1 - t, 4)
    peers = peers + jnp.where((t == cross) | (t == cross + 1), RELAYS, 0) + jnp.where(is_relay, 2, 0)
    pl.semaphore_wait(barrier, peers)
    order = [2 * f + j for f in reversed(range(frames)) for j in range(2)]
    for k in order[:1]:
        to_x(k).start()
    for f in reversed(range(frames)):
        to_sibling(f).start()
    for dt in range(3):
        w_copy(dt).start()

    for f in range(frames):
        own_copy(f).wait()
    count = float(PER_GROUP * rows * cols)

    def sums(f, _):
        for g in range(groups):
            x = raw_own[f, g * PER_GROUP : (g + 1) * PER_GROUP].astype(F32)
            srow[pl.ds(f * groups + g, 1), :] = jnp.sum(jnp.sum(x, axis=0), axis=0, keepdims=True)
        return _

    lax.fori_loop(0, frames, sums, 0)
    mrow[...] = jnp.broadcast_to(jnp.sum(srow[...], axis=1, keepdims=True) / count, mrow.shape)

    def squares(f, _):
        for g in range(groups):
            x = raw_own[f, g * PER_GROUP : (g + 1) * PER_GROUP].astype(F32)
            d = x - mrow[pl.ds(f * groups + g, 1), :][None]
            srow[pl.ds(f * groups + g, 1), :] = jnp.sum(jnp.sum(d * d, axis=0), axis=0, keepdims=True)
        return _

    lax.fori_loop(0, frames, squares, 0)
    sq = jnp.broadcast_to(jnp.sum(srow[...], axis=1, keepdims=True), srow.shape)
    lane = lax.broadcasted_iota(jnp.int32, (groups, cols), 1)
    message = jnp.zeros((groups, cols), F32)
    for f in range(frames):
        here = slice(f * groups, (f + 1) * groups)
        message = jnp.where(lane // 16 == f, mrow[here, :], message)
        message = jnp.where(lane // 16 == frames + f, sq[here], message)
    stat[8] = message
    for i, hop in enumerate(HOPS):

        @pl.when((t + hop >= 0) & (t + hop < tiles))
        def _():
            send_stat(i).start()

    for k in order[1:3]:
        to_x(k).start()


    for copy in small:
        copy.wait()

    first = t * frames

    def bounds(k, carry):
        end, starts, ends = carry
        end = end + lens[k]
        starts = tuple(jnp.where(end <= first + f, end, starts[f]) for f in range(frames))
        ends = tuple(jnp.where(end > first + f, jnp.minimum(ends[f], end), ends[f]) for f in range(frames))
        return end, starts, ends

    zero = jnp.int32(0)
    _, starts, ends = lax.fori_loop(
        0, lens.shape[0], bounds, (zero, (zero,) * frames, (jnp.int32(1 << 20),) * frames)
    )
    for f in range(frames):
        for dt in range(3):
            msk[f * 3 + dt] = jnp.where(first + f + 2 - dt < ends[f], 1.0, 0.0).astype(F32)

    def spread_rows(k, _):
        par[0, pl.ds(k, 1), :] = jnp.full((1, cols), gain[k], F32)
        par[1, pl.ds(k, 1), :] = jnp.full((1, cols), shift[k], F32)
        par[2, pl.ds(k, 1), :] = jnp.full((1, cols), bias[k], F32)
        return _

    lax.fori_loop(0, chans, spread_rows, 0)
    swap[...] = swap_matrix()

    for part in range(2):
        acc[frames + part] = jnp.zeros((rows, chans, cols), F32)

    all_runs = tuple(range(chans // 16))

    def tiles_of(ref, at, runs=all_runs):
        return jnp.concatenate([ref[(*at, pl.ds(16 * j, 16))].reshape(256, cols) for j in runs], axis=1)

    def begin(f, _):
        y = jnp.dot(swap[...], tiles_of(raw_own, (f,)), preferred_element_type=F32)
        for j in range(chans // 16):
            here = slice(16 * j, 16 * (j + 1))
            acc[f, :, here, :] = y[:, j * cols : (j + 1) * cols].reshape(rows, 16, cols) + par[2, here, :][None]
        return _

    lax.fori_loop(0, frames, begin, 0)

    for dt in range(3):
        w_copy(dt).wait()
        for q in range(2):
            for tap in range(9):
                wt[q, dt * chans : (dt + 1) * chans, tap * 2 * chans : (tap + 1) * 2 * chans] = slab[
                    dt, tap, :, q * 2 * chans : (q + 1) * 2 * chans
                ]

    for hid in (hid_a, hid_b):
        hid[0:row_k, :] = jnp.zeros((row_k, cols), BF16)
        hid[17 * row_k : 18 * row_k, :] = jnp.zeros((row_k, cols), BF16)

    for i, hop in enumerate(HOPS):

        @pl.when((t - hop >= 0) & (t - hop < tiles))
        def _():
            send_stat(i).wait_recv()

    lane_frame = (lane // 16) % frames
    is_mean = lane // 16 < frames
    scales = jnp.zeros((chans, cols), F32)
    lane_c = lax.broadcasted_iota(jnp.int32, (chans, cols), 1)
    row8 = lax.broadcasted_iota(jnp.int32, (8, cols), 0)

    def per_channel(v):
        blocks = []
        for b in range(chans // 8):
            g0, g1 = (8 * b) // PER_GROUP, (8 * b + 7) // PER_GROUP
            lo = jnp.broadcast_to(v[g0 : g0 + 1], (8, cols))
            if g1 != g0:
                lo = jnp.where(row8 < (g0 + 1) * PER_GROUP - 8 * b, lo, jnp.broadcast_to(v[g1 : g1 + 1], (8, cols)))
            blocks.append(lo)
        return jnp.concatenate(blocks, axis=0)

    hops = (*HOPS, 0)
    for f in range(frames):
        inside = []
        for h in hops:
            at = (t - h) * frames + lane_frame
            inside.append((at >= starts[f]) & (at < ends[f]))
        length = (ends[f] - starts[f]).astype(F32)
        total = jnp.zeros((groups, cols), F32)
        for i in range(9):
            total = total + jnp.where(inside[i] & is_mean, stat[i], 0.0)
        mean = jnp.sum(total, axis=1, keepdims=True) / (16.0 * length)
        total = jnp.zeros((groups, cols), F32)
        for i in range(9):
            d = stat[i] - mean
            total = total + jnp.where(inside[i], jnp.where(is_mean, d * d, stat[i] * (1.0 / count)), 0.0)
        spread = jnp.sum(total, axis=1, keepdims=True) / (16.0 * length)
        rstd = lax.rsqrt(spread + EPS)
        a = 0.5 * (per_channel(jnp.broadcast_to(rstd, (groups, cols))) * par[0])
        b = 0.5 * par[1] - per_channel(jnp.broadcast_to(mean, (groups, cols))) * a
        ab[0, 0, f] = a
        ab[0, 1, f] = b
        scales = jnp.where(lane_c // 16 == f, a, scales)
        scales = jnp.where(lane_c // 16 == frames + f, b, scales)
    abmsg[0] = scales
    for r in (2, 3, 1):
        send_ab(r).start()
    for k in order[3:6]:
        to_x(k).start()

    def expand(r):
        for f in range(frames):
            ab[r, 0, f] = jnp.broadcast_to(abmsg[r, :, 16 * f : 16 * f + 1], (chans, cols))
            lo = 16 * (frames + f)
            ab[r, 1, f] = jnp.broadcast_to(abmsg[r, :, lo : lo + 1], (chans, cols))

    lane_t = lax.broadcasted_iota(jnp.int32, (16, cols), 1)

    def normalize(slot, f, hid, runs=all_runs):
        place = slot % 2 + (1 - 2 * (slot % 2)) * (c % 2)
        raw = (raw_own, raw_sib, raw_x, raw_xs)[slot]
        y = jnp.dot(swap[...], tiles_of(raw, (f,), runs), preferred_element_type=F32)
        for i, j in enumerate(runs):
            here = slice(16 * j, 16 * (j + 1))
            a, b = ab[slot, 0, f, here, :], ab[slot, 1, f, here, :]
            for h in range(rows):
                z = y[h * 16 : (h + 1) * 16, i * cols : (i + 1) * cols] * a + b
                z = z + z * jnp.tanh(z)
                left = jnp.where(lane_t == 0, 0.0, pltpu.roll(z, 1, 1))
                right = jnp.where(lane_t == cols - 1, 0.0, pltpu.roll(z, cols - 1, 1))
                for dw, piece in enumerate((left, z, right)):
                    to = pl.multiple_of(((h + 1) * 3 + dw) * 2 * chans + place * chans + 16 * j, 16)
                    hid[pl.ds(to, 16), :] = piece.astype(BF16)

    def convolve(q, f, hid, first_row, n):
        pieces = [hid[pl.ds(pl.multiple_of((first_row + j) * row_k, row_k), kdim), :] for j in range(n)]
        res = jnp.dot(wt[q], jnp.concatenate(pieces, axis=1), preferred_element_type=F32)
        for dt in range(3):
            m = msk[f * 3 + dt]
            for j in range(n):
                part = res[dt * chans : (dt + 1) * chans, j * cols : (j + 1) * cols]
                acc[f + 2 - dt, first_row + j] += part * m

    def stage(conv, norms):
        n = rows // 2
        for p in range(2):
            if conv is not None:
                q, f = conv
                convolve(q + (1 - 2 * q) * (c // 2), f, hid_of[conv], p * n, n)
            for slot, f, runs in norms[p]:
                normalize(slot, f, hid_of[slot // 2, f], runs)

    def both(q, f):
        return [(2 * q, f, all_runs)], [(2 * q + 1, f, all_runs)]

    def finish(f):
        pieces = []
        for j in range(chans // 16):
            here = slice(16 * j, 16 * (j + 1))
            value = acc[f, :, here, :]
            pieces.append(value.astype(BF16).reshape(256, cols))
        y = jnp.dot(swap[...], jnp.concatenate(pieces, axis=1), preferred_element_type=F32).astype(BF16)
        for j in range(chans // 16):
            out[f, 16 * j : 16 * (j + 1)] = y[:, j * cols : (j + 1) * cols].reshape(16, rows, cols)

    def arrived(k):
        to_x(k).wait_recv()
        forward(k).start()

    def send_halo(i):
        @pl.when(t < tiles - 1)
        def _():
            pout[i] = acc[frames + i].astype(BF16)

        @pl.when((t < tiles - 1) & (t != cross))
        def _():
            send_part(i).start()

        @pl.when(t == cross)
        def _():
            for j in range(RELAYS):
                to_relay(i, j).start()

    def relay_halo(i):
        @pl.when(is_relay)
        def _():
            to_relay(i, 0).wait_recv()
            from_relay(i, my_share).start()

    def take_halo(i):
        @pl.when((t > 0) & (t != cross + 1))
        def _():
            send_part(i).wait_recv()

        @pl.when(t == cross + 1)
        def _():
            for j in range(RELAYS):
                from_relay(i, j).wait_recv()

        @pl.when(t > 0)
        def _():
            acc[i] += pin[i].astype(F32)

    own, rem = 0, 1
    steps = [(own, 3), (own, 2), (rem, 3), (own, 1), (rem, 2), (own, 0), (rem, 1), (rem, 0)]
    hid_of = {step: (hid_a, hid_b)[i % 2] for i, step in enumerate(steps)}

    low, high = all_runs[: len(all_runs) // 2], all_runs[len(all_runs) // 2 :]
    none = [], []
    send_ab(1).wait_recv()
    expand(1)
    for f in range(frames):
        to_sibling(f).wait_recv()
    stage(None, both(own, 3))
    arrived(6)
    stage((own, 3), both(own, 2))
    arrived(7)
    send_ab(2).wait_recv()
    expand(2)
    send_ab(3).wait_recv()
    expand(3)
    for k in (6, 7):
        forward(k).wait_recv()
    stage((own, 2), both(rem, 3))
    arrived(4)
    stage((rem, 3), both(own, 1))
    send_halo(1)
    to_x(order[6]).start()
    arrived(5)
    for k in (4, 5):
        forward(k).wait_recv()
    stage((own, 1), both(rem, 2))
    stage((rem, 2), both(own, 0))
    send_halo(0)
    relay_halo(1)
    to_x(order[7]).start()
    arrived(2)
    arrived(3)
    for k in (2, 3):
        forward(k).wait_recv()
    stage((own, 0), both(rem, 1))
    arrived(0)
    stage((rem, 1), ([(2, 0, low)], []))
    arrived(1)
    relay_halo(0)
    finish(3)
    forward(0).wait_recv()
    stage(None, ([(3, 0, low)], [(2, 0, high)]))
    forward(1).wait_recv()
    stage(None, ([(3, 0, high)], []))
    stage((rem, 0), none)
    finish(2)
    take_halo(1)
    finish(1)
    take_halo(0)
    finish(0)

    for i in range(2):

        @pl.when((t < tiles - 1) & (t != cross))
        def _():
            send_part(i).wait_send()

        @pl.when(t == cross)
        def _():
            for j in range(RELAYS):
                to_relay(i, j).wait_send()

        @pl.when(is_relay)
        def _():
            from_relay(i, my_share).wait_send()

    for f in range(frames):
        to_sibling(f).wait_send()
    for k in order:
        to_x(k).wait_send()
        forward(k).wait_send()
    for i, hop in enumerate(HOPS):

        @pl.when((t + hop >= 0) & (t + hop < tiles))
        def _():
            send_stat(i).wait_send()

    for r in (1, 2, 3):
        send_ab(r).wait_send()


def on_device(video, clip_lengths, norm_gain, norm_shift, conv_weight, conv_bias):
    frames, chans, rows, cols = video.shape
    groups = chans // PER_GROUP
    all_chans = conv_weight.shape[3]
    weight = jnp.swapaxes(conv_weight, 3, 4).reshape(3, 9, chans, all_chans)
    dma = pltpu.SemaphoreType.DMA
    anyspace = pl.BlockSpec(memory_space=pltpu.HBM)
    return pl.pallas_call(
        kernel,
        out_shape=jax.ShapeDtypeStruct(video.shape, BF16),
        in_specs=[anyspace] * 6,
        out_specs=pl.BlockSpec(memory_space=pltpu.VMEM),
        scratch_shapes=[
            pltpu.VMEM((frames, chans, rows, cols), BF16),
            pltpu.VMEM((frames, chans, rows, cols), BF16),
            pltpu.VMEM((frames, chans, rows, cols), BF16),
            pltpu.VMEM((frames, chans, rows, cols), BF16),
            pltpu.VMEM((3, 9, chans, 4 * chans), BF16),
            pltpu.VMEM((2, 3 * chans, 18 * chans), BF16),
            pltpu.VMEM((18 * 6 * chans, cols), BF16),
            pltpu.VMEM((18 * 6 * chans, cols), BF16),
            pltpu.VMEM((frames + 2, rows, chans, cols), F32),
            pltpu.VMEM((2, rows, chans, cols), BF16),
            pltpu.VMEM((2, rows, chans, cols), BF16),
            pltpu.VMEM((2, rows // RELAYS, chans, cols), BF16),
            pltpu.VMEM((4, 2, frames, chans, cols), F32),
            pltpu.VMEM((4, chans, cols), F32),
            pltpu.VMEM((3, chans, cols), F32),
            pltpu.VMEM((256, 256), BF16),
            pltpu.VMEM((frames * groups, cols), F32),
            pltpu.VMEM((frames * groups, cols), F32),
            pltpu.VMEM((9, groups, cols), F32),
            pltpu.SMEM((3 * frames,), F32),
            pltpu.SMEM(clip_lengths.shape, jnp.int32),
            pltpu.SMEM((chans,), F32),
            pltpu.SMEM((chans,), F32),
            pltpu.SMEM((chans,), F32),
            dma((4,)),
            dma((frames,)), dma((3,)),
            dma((2 * frames,)), dma((2 * frames,)), dma((frames,)), dma((frames,)), dma((2 * frames,)), dma((2 * frames,)),
            dma((8,)), dma((8,)), dma((4,)), dma((4,)), dma((2,)), dma((2,)),
            dma((2, RELAYS)), dma((2,)), dma((2,)), dma((2, RELAYS)),
        ],
        compiler_params=pltpu.CompilerParams(
            collective_id=0, has_side_effects=True, vmem_limit_bytes=58 << 20
        ),
        name="resblock",
    )(clip_lengths, norm_gain, norm_shift, conv_bias, video, weight)


def solution(mesh):
    return jax.shard_map(
        on_device,
        mesh=mesh,
        in_specs=(
            P("tile", "chan", None, None),
            P(),
            P("chan"),
            P("chan"),
            P(None, None, None, None, "chan"),
            P("chan"),
        ),
        out_specs=P("tile", "chan", None, None),
        check_vma=False,
    )
```

```python
import jax
import jax.numpy as jnp
from jax import lax
from jax.experimental import pallas as pl
from jax.experimental.pallas import tpu as pltpu
from jax.sharding import PartitionSpec as P

MESH = pl.DeviceIdType.MESH
F32 = jnp.float32
BF16 = jnp.bfloat16
PER_GROUP = 12
HOPS = (1, -1, 2, -2, 3, -3, 4, -4)
EPS = 1e-06
RELAYS = 8


def swap_matrix():
    row = lax.broadcasted_iota(jnp.int32, (256, 256), 0)
    col = lax.broadcasted_iota(jnp.int32, (256, 256), 1)
    return jnp.where(col == (row % 16) * 16 + row // 16, 1.0, 0.0).astype(BF16)


def kernel(
    lens_in, gain_in, shift_in, bias_in, video, weight, out,
    raw_own, raw_sib, raw_x, raw_xs, slab, wt, hid_a, hid_b, acc, pout, pin, hop_buf, ab, abmsg, par, swap, srow, mrow, stat, msk, lens, gain, shift, bias, par_sem,
    own_sem, w_sem, xs, xr, ss, sr, fs, fr, ts, tr, cs, cr, ps, pr, hs, hr, qs, qr,
):
    frames, chans, rows, cols = video.shape
    groups = chans // PER_GROUP
    half = chans // 2
    kdim = 9 * 2 * chans
    row_k = 3 * 2 * chans
    t, c = lax.axis_index("tile"), lax.axis_index("chan")
    tiles = lax.axis_size("tile")

    def tile_at(hop):
        return (lax.rem(t + hop + tiles, tiles), c)

    def mate(r):
        return (t, c + r - 2 * (c % 2) if r == 1 else c + 2 - 4 * (c // 2) if r == 2 else 3 - c)

    def remote(src, dst, send, recv, dev):
        return pltpu.make_async_remote_copy(
            src_ref=src, dst_ref=dst, send_sem=send, recv_sem=recv, device_id=dev, device_id_type=MESH
        )

    def half_frame(k):
        return pl.ds((k % 2) * half, half)

    def to_x(k):
        f, here = k // 2, half_frame(k)
        return remote(video.at[f, here], raw_x.at[f, here], xs.at[k], xr.at[k], mate(2))

    def to_sibling(f):
        return remote(video.at[f], raw_sib.at[f], ss.at[f], sr.at[f], mate(1))

    def forward(k):
        f, here = k // 2, half_frame(k)
        return remote(raw_x.at[f, here], raw_xs.at[f, here], fs.at[k], fr.at[k], mate(1))

    def send_stat(i):
        return remote(stat.at[8], stat.at[i], ts.at[i], tr.at[i], tile_at(HOPS[i]))

    def send_ab(r):
        return remote(abmsg.at[0], abmsg.at[r], cs.at[r], cr.at[r], mate(r))

    def send_part(i):
        return remote(pout.at[i], pin.at[i], ps.at[i], pr.at[i], (lax.rem(t + 1, tiles), c))

    cross = tiles // 2 - 1
    is_relay = ((t % 2 == 1) & (t < cross)) | (t == cross - 1)
    my_share = t // 2
    share = rows // RELAYS

    def relay(j):
        return (2 * j + 1 if j < RELAYS - 1 else cross - 1, c)

    def to_relay(i, j):
        src = pout.at[i, pl.ds(j * share, share)]
        return remote(src, hop_buf.at[i], hs.at[i, j], hr.at[i], relay(j))

    def from_relay(i, j):
        dst = pin.at[i, pl.ds(j * share, share)]
        return remote(hop_buf.at[i], dst, qs.at[i], qr.at[i, j], (cross + 1, c))

    def own_copy(f):
        return pltpu.make_async_copy(video.at[f], raw_own.at[f], own_sem.at[f])

    def w_copy(dt):
        return pltpu.make_async_copy(weight.at[dt], slab.at[dt], w_sem.at[dt])

    small = [
        pltpu.make_async_copy(src, dst, par_sem.at[i])
        for i, (src, dst) in enumerate(((lens_in, lens), (gain_in, gain), (shift_in, shift), (bias_in, bias)))
    ]
    for f in range(frames):
        own_copy(f).start()
    for copy in small:
        copy.start()
    barrier = pltpu.get_barrier_semaphore()
    for r in (2, 1, 3):
        pl.semaphore_signal(barrier, inc=1, device_id=mate(r), device_id_type=MESH)
    for hop in HOPS:

        @pl.when((t + hop >= 0) & (t + hop < tiles))
        def _():
            pl.semaphore_signal(barrier, inc=1, device_id=tile_at(hop), device_id_type=MESH)

    @pl.when((t == cross) | (t == cross + 1))
    def _():
        for j in range(RELAYS):
            pl.semaphore_signal(barrier, inc=1, device_id=relay(j), device_id_type=MESH)

    @pl.when(is_relay)
    def _():
        for d in (cross, cross + 1):
            pl.semaphore_signal(barrier, inc=1, device_id=(d, c), device_id_type=MESH)

    peers = 3 + jnp.minimum(t, 4) + jnp.minimum(tiles - 1 - t, 4)
    peers = peers + jnp.where((t == cross) | (t == cross + 1), RELAYS, 0) + jnp.where(is_relay, 2, 0)
    pl.semaphore_wait(barrier, peers)
    order = [2 * f + j for f in reversed(range(frames)) for j in range(2)]
    for k in order[:1]:
        to_x(k).start()
    for f in reversed(range(frames)):
        to_sibling(f).start()
    for dt in range(3):
        w_copy(dt).start()

    for f in range(frames):
        own_copy(f).wait()
    count = float(PER_GROUP * rows * cols)

    def sums(f, _):
        for g in range(groups):
            x = raw_own[f, g * PER_GROUP : (g + 1) * PER_GROUP].astype(F32)
            srow[pl.ds(f * groups + g, 1), :] = jnp.sum(jnp.sum(x, axis=0), axis=0, keepdims=True)
        return _

    lax.fori_loop(0, frames, sums, 0)
    mrow[...] = jnp.broadcast_to(jnp.sum(srow[...], axis=1, keepdims=True) / count, mrow.shape)

    def squares(f, _):
        for g in range(groups):
            x = raw_own[f, g * PER_GROUP : (g + 1) * PER_GROUP].astype(F32)
            d = x - mrow[pl.ds(f * groups + g, 1), :][None]
            srow[pl.ds(f * groups + g, 1), :] = jnp.sum(jnp.sum(d * d, axis=0), axis=0, keepdims=True)
        return _

    lax.fori_loop(0, frames, squares, 0)
    sq = jnp.broadcast_to(jnp.sum(srow[...], axis=1, keepdims=True), srow.shape)
    lane = lax.broadcasted_iota(jnp.int32, (groups, cols), 1)
    message = jnp.zeros((groups, cols), F32)
    for f in range(frames):
        here = slice(f * groups, (f + 1) * groups)
        message = jnp.where(lane // 16 == f, mrow[here, :], message)
        message = jnp.where(lane // 16 == frames + f, sq[here], message)
    stat[8] = message
    for i, hop in enumerate(HOPS):

        @pl.when((t + hop >= 0) & (t + hop < tiles))
        def _():
            send_stat(i).start()

    for k in order[1:3]:
        to_x(k).start()


    for copy in small:
        copy.wait()

    first = t * frames

    def bounds(k, carry):
        end, starts, ends = carry
        end = end + lens[k]
        starts = tuple(jnp.where(end <= first + f, end, starts[f]) for f in range(frames))
        ends = tuple(jnp.where(end > first + f, jnp.minimum(ends[f], end), ends[f]) for f in range(frames))
        return end, starts, ends

    zero = jnp.int32(0)
    _, starts, ends = lax.fori_loop(
        0, lens.shape[0], bounds, (zero, (zero,) * frames, (jnp.int32(1 << 20),) * frames)
    )
    for f in range(frames):
        for dt in range(3):
            msk[f * 3 + dt] = jnp.where(first + f + 2 - dt < ends[f], 1.0, 0.0).astype(F32)

    def spread_rows(k, _):
        par[0, pl.ds(k, 1), :] = jnp.full((1, cols), gain[k], F32)
        par[1, pl.ds(k, 1), :] = jnp.full((1, cols), shift[k], F32)
        par[2, pl.ds(k, 1), :] = jnp.full((1, cols), bias[k], F32)
        return _

    lax.fori_loop(0, chans, spread_rows, 0)
    swap[...] = swap_matrix()

    for part in range(2):
        acc[frames + part] = jnp.zeros((rows, chans, cols), F32)

    all_runs = tuple(range(chans // 16))

    def tiles_of(ref, at, runs=all_runs):
        return jnp.concatenate([ref[(*at, pl.ds(16 * j, 16))].reshape(256, cols) for j in runs], axis=1)

    def begin(f, _):
        y = jnp.dot(swap[...], tiles_of(raw_own, (f,)), preferred_element_type=F32)
        for j in range(chans // 16):
            here = slice(16 * j, 16 * (j + 1))
            acc[f, :, here, :] = y[:, j * cols : (j + 1) * cols].reshape(rows, 16, cols) + par[2, here, :][None]
        return _

    lax.fori_loop(0, frames, begin, 0)

    for dt in range(3):
        w_copy(dt).wait()
        for q in range(2):
            for tap in range(9):
                wt[q, dt * chans : (dt + 1) * chans, tap * 2 * chans : (tap + 1) * 2 * chans] = slab[
                    dt, tap, :, q * 2 * chans : (q + 1) * 2 * chans
                ]

    for hid in (hid_a, hid_b):
        hid[0:row_k, :] = jnp.zeros((row_k, cols), BF16)
        hid[17 * row_k : 18 * row_k, :] = jnp.zeros((row_k, cols), BF16)

    for i, hop in enumerate(HOPS):

        @pl.when((t - hop >= 0) & (t - hop < tiles))
        def _():
            send_stat(i).wait_recv()

    lane_frame = (lane // 16) % frames
    is_mean = lane // 16 < frames
    scales = jnp.zeros((chans, cols), F32)
    lane_c = lax.broadcasted_iota(jnp.int32, (chans, cols), 1)
    row8 = lax.broadcasted_iota(jnp.int32, (8, cols), 0)

    def per_channel(v):
        blocks = []
        for b in range(chans // 8):
            g0, g1 = (8 * b) // PER_GROUP, (8 * b + 7) // PER_GROUP
            lo = jnp.broadcast_to(v[g0 : g0 + 1], (8, cols))
            if g1 != g0:
                lo = jnp.where(row8 < (g0 + 1) * PER_GROUP - 8 * b, lo, jnp.broadcast_to(v[g1 : g1 + 1], (8, cols)))
            blocks.append(lo)
        return jnp.concatenate(blocks, axis=0)

    hops = (*HOPS, 0)
    for f in range(frames):
        inside = []
        for h in hops:
            at = (t - h) * frames + lane_frame
            inside.append((at >= starts[f]) & (at < ends[f]))
        length = (ends[f] - starts[f]).astype(F32)
        total = jnp.zeros((groups, cols), F32)
        for i in range(9):
            total = total + jnp.where(inside[i] & is_mean, stat[i], 0.0)
        mean = jnp.sum(total, axis=1, keepdims=True) / (16.0 * length)
        total = jnp.zeros((groups, cols), F32)
        for i in range(9):
            d = stat[i] - mean
            total = total + jnp.where(inside[i], jnp.where(is_mean, d * d, stat[i] * (1.0 / count)), 0.0)
        spread = jnp.sum(total, axis=1, keepdims=True) / (16.0 * length)
        rstd = lax.rsqrt(spread + EPS)
        a = 0.5 * (per_channel(jnp.broadcast_to(rstd, (groups, cols))) * par[0])
        b = 0.5 * par[1] - per_channel(jnp.broadcast_to(mean, (groups, cols))) * a
        ab[0, 0, f] = a
        ab[0, 1, f] = b
        scales = jnp.where(lane_c // 16 == f, a, scales)
        scales = jnp.where(lane_c // 16 == frames + f, b, scales)
    abmsg[0] = scales
    for r in (2, 3, 1):
        send_ab(r).start()
    for k in order[3:6]:
        to_x(k).start()

    def expand(r):
        for f in range(frames):
            ab[r, 0, f] = jnp.broadcast_to(abmsg[r, :, 16 * f : 16 * f + 1], (chans, cols))
            lo = 16 * (frames + f)
            ab[r, 1, f] = jnp.broadcast_to(abmsg[r, :, lo : lo + 1], (chans, cols))

    lane_t = lax.broadcasted_iota(jnp.int32, (16, cols), 1)

    def normalize(slot, f, hid, runs=all_runs):
        place = slot % 2 + (1 - 2 * (slot % 2)) * (c % 2)
        raw = (raw_own, raw_sib, raw_x, raw_xs)[slot]
        y = jnp.dot(swap[...], tiles_of(raw, (f,), runs), preferred_element_type=F32)
        for i, j in enumerate(runs):
            here = slice(16 * j, 16 * (j + 1))
            a, b = ab[slot, 0, f, here, :], ab[slot, 1, f, here, :]
            for h in range(rows):
                z = y[h * 16 : (h + 1) * 16, i * cols : (i + 1) * cols] * a + b
                z = z + z * jnp.tanh(z)
                left = jnp.where(lane_t == 0, 0.0, pltpu.roll(z, 1, 1))
                right = jnp.where(lane_t == cols - 1, 0.0, pltpu.roll(z, cols - 1, 1))
                for dw, piece in enumerate((left, z, right)):
                    to = pl.multiple_of(((h + 1) * 3 + dw) * 2 * chans + place * chans + 16 * j, 16)
                    hid[pl.ds(to, 16), :] = piece.astype(BF16)

    def convolve(q, f, hid, first_row, n):
        pieces = [hid[pl.ds(pl.multiple_of((first_row + j) * row_k, row_k), kdim), :] for j in range(n)]
        res = jnp.dot(wt[q], jnp.concatenate(pieces, axis=1), preferred_element_type=F32)
        for dt in range(3):
            m = msk[f * 3 + dt]
            for j in range(n):
                part = res[dt * chans : (dt + 1) * chans, j * cols : (j + 1) * cols]
                acc[f + 2 - dt, first_row + j] += part * m

    def stage(conv, norms):
        n = rows // 2
        for p in range(2):
            if conv is not None:
                q, f = conv
                convolve(q + (1 - 2 * q) * (c // 2), f, hid_of[conv], p * n, n)
            for slot, f, runs in norms[p]:
                normalize(slot, f, hid_of[slot // 2, f], runs)

    def both(q, f):
        return [(2 * q, f, all_runs)], [(2 * q + 1, f, all_runs)]

    def finish(f):
        pieces = []
        for j in range(chans // 16):
            here = slice(16 * j, 16 * (j + 1))
            value = acc[f, :, here, :]
            pieces.append(value.astype(BF16).reshape(256, cols))
        y = jnp.dot(swap[...], jnp.concatenate(pieces, axis=1), preferred_element_type=F32).astype(BF16)
        for j in range(chans // 16):
            out[f, 16 * j : 16 * (j + 1)] = y[:, j * cols : (j + 1) * cols].reshape(16, rows, cols)

    def arrived(k):
        to_x(k).wait_recv()
        forward(k).start()

    def send_halo(i):
        @pl.when(t < tiles - 1)
        def _():
            pout[i] = acc[frames + i].astype(BF16)

        @pl.when((t < tiles - 1) & (t != cross))
        def _():
            send_part(i).start()

        @pl.when(t == cross)
        def _():
            for j in range(RELAYS):
                to_relay(i, j).start()

    def relay_halo(i):
        @pl.when(is_relay)
        def _():
            to_relay(i, 0).wait_recv()
            from_relay(i, my_share).start()

    def take_halo(i):
        @pl.when((t > 0) & (t != cross + 1))
        def _():
            send_part(i).wait_recv()

        @pl.when(t == cross + 1)
        def _():
            for j in range(RELAYS):
                from_relay(i, j).wait_recv()

        @pl.when(t > 0)
        def _():
            acc[i] += pin[i].astype(F32)

    own, rem = 0, 1
    steps = [(own, 3), (own, 2), (rem, 3), (own, 1), (rem, 2), (own, 0), (rem, 1), (rem, 0)]
    hid_of = {step: (hid_a, hid_b)[i % 2] for i, step in enumerate(steps)}

    low, high = all_runs[: len(all_runs) // 2], all_runs[len(all_runs) // 2 :]
    none = [], []
    send_ab(1).wait_recv()
    expand(1)
    for f in range(frames):
        to_sibling(f).wait_recv()
    stage(None, both(own, 3))
    arrived(6)
    stage((own, 3), both(own, 2))
    arrived(7)
    send_ab(2).wait_recv()
    expand(2)
    send_ab(3).wait_recv()
    expand(3)
    for k in (6, 7):
        forward(k).wait_recv()
    stage((own, 2), both(rem, 3))
    arrived(4)
    stage((rem, 3), both(own, 1))
    send_halo(1)
    to_x(order[6]).start()
    arrived(5)
    for k in (4, 5):
        forward(k).wait_recv()
    stage((own, 1), both(rem, 2))
    stage((rem, 2), both(own, 0))
    send_halo(0)
    relay_halo(1)
    to_x(order[7]).start()
    arrived(2)
    arrived(3)
    for k in (2, 3):
        forward(k).wait_recv()
    stage((own, 0), both(rem, 1))
    arrived(0)
    stage((rem, 1), ([(2, 0, low)], []))
    arrived(1)
    relay_halo(0)
    finish(3)
    forward(0).wait_recv()
    stage(None, ([(3, 0, low)], [(2, 0, high)]))
    forward(1).wait_recv()
    stage(None, ([(3, 0, high)], []))
    stage((rem, 0), none)
    finish(2)
    take_halo(1)
    finish(1)
    take_halo(0)
    finish(0)

    for i in range(2):

        @pl.when((t < tiles - 1) & (t != cross))
        def _():
            send_part(i).wait_send()

        @pl.when(t == cross)
        def _():
            for j in range(RELAYS):
                to_relay(i, j).wait_send()

        @pl.when(is_relay)
        def _():
            from_relay(i, my_share).wait_send()

    for f in range(frames):
        to_sibling(f).wait_send()
    for k in order:
        to_x(k).wait_send()
        forward(k).wait_send()
    for i, hop in enumerate(HOPS):

        @pl.when((t + hop >= 0) & (t + hop < tiles))
        def _():
            send_stat(i).wait_send()

    for r in (1, 2, 3):
        send_ab(r).wait_send()


def on_device(video, clip_lengths, norm_gain, norm_shift, conv_weight, conv_bias):
    frames, chans, rows, cols = video.shape
    groups = chans // PER_GROUP
    all_chans = conv_weight.shape[3]
    weight = jnp.swapaxes(conv_weight, 3, 4).reshape(3, 9, chans, all_chans)
    dma = pltpu.SemaphoreType.DMA
    anyspace = pl.BlockSpec(memory_space=pltpu.HBM)
    return pl.pallas_call(
        kernel,
        out_shape=jax.ShapeDtypeStruct(video.shape, BF16),
        in_specs=[anyspace] * 6,
        out_specs=pl.BlockSpec(memory_space=pltpu.VMEM),
        scratch_shapes=[
            pltpu.VMEM((frames, chans, rows, cols), BF16),
            pltpu.VMEM((frames, chans, rows, cols), BF16),
            pltpu.VMEM((frames, chans, rows, cols), BF16),
            pltpu.VMEM((frames, chans, rows, cols), BF16),
            pltpu.VMEM((3, 9, chans, 4 * chans), BF16),
            pltpu.VMEM((2, 3 * chans, 18 * chans), BF16),
            pltpu.VMEM((18 * 6 * chans, cols), BF16),
            pltpu.VMEM((18 * 6 * chans, cols), BF16),
            pltpu.VMEM((frames + 2, rows, chans, cols), F32),
            pltpu.VMEM((2, rows, chans, cols), BF16),
            pltpu.VMEM((2, rows, chans, cols), BF16),
            pltpu.VMEM((2, rows // RELAYS, chans, cols), BF16),
            pltpu.VMEM((4, 2, frames, chans, cols), F32),
            pltpu.VMEM((4, chans, cols), F32),
            pltpu.VMEM((3, chans, cols), F32),
            pltpu.VMEM((256, 256), BF16),
            pltpu.VMEM((frames * groups, cols), F32),
            pltpu.VMEM((frames * groups, cols), F32),
            pltpu.VMEM((9, groups, cols), F32),
            pltpu.SMEM((3 * frames,), F32),
            pltpu.SMEM(clip_lengths.shape, jnp.int32),
            pltpu.SMEM((chans,), F32),
            pltpu.SMEM((chans,), F32),
            pltpu.SMEM((chans,), F32),
            dma((4,)),
            dma((frames,)), dma((3,)),
            dma((2 * frames,)), dma((2 * frames,)), dma((frames,)), dma((frames,)), dma((2 * frames,)), dma((2 * frames,)),
            dma((8,)), dma((8,)), dma((4,)), dma((4,)), dma((2,)), dma((2,)),
            dma((2, RELAYS)), dma((2,)), dma((2,)), dma((2, RELAYS)),
        ],
        compiler_params=pltpu.CompilerParams(
            collective_id=0, has_side_effects=True, vmem_limit_bytes=52 << 20
        ),
        name="resblock",
    )(clip_lengths, norm_gain, norm_shift, conv_bias, video, weight)


def solution(mesh):
    return jax.shard_map(
        on_device,
        mesh=mesh,
        in_specs=(
            P("tile", "chan", None, None),
            P(),
            P("chan"),
            P("chan"),
            P(None, None, None, None, "chan"),
            P("chan"),
        ),
        out_specs=P("tile", "chan", None, None),
        check_vma=False,
    )
```
